256 devices in a mesh: section: 8 (over x_lo, y), shard: 32 (over z, x_hi, core).
Axes of the slice: x: 4 (x_hi: 2, x_lo: 2; x = x_hi * 2 + x_lo), y: 4, z: 8, core: 2. Of those that a mesh axis runs over, the one named last changes fastest.
Arguments:
- states: bfloat16 [2048, 8192], P('section', 'shard'), may hold values from -6 to 6
- lengths: int32 [8], replicated, may hold values from 64 to 256, as said below
- gate_weight: bfloat16 [8192, 14336], P(('section', 'shard')), may hold values from -0.0625 to 0.0625
- up_weight: bfloat16 [8192, 14336], P(('section', 'shard')), may hold values from -0.0625 to 0.0625
- upstream: bfloat16 [2048, 14336], P('section', 'shard'), may hold values from -6 to 6
Outputs:
- hidden: bfloat16 [2048, 14336], P('section', 'shard')
- new_gate: bfloat16 [8192, 14336], P('section', 'shard')
- new_up: bfloat16 [8192, 14336], P('section', 'shard')
The draws below stay inside these ranges and needn't reach their ends.
Inputs may be any that keep to these rules, and one draw needn't show every extreme that they name: `lengths`: some rollout has length exactly 256.
All inputs are finite; a program needn't handle non-finite values.
Results may differ from the reference program's by a relative error of at most 0.015.
Values may be sent and summed in bfloat16 or wider, within the bound.
A program may use at most 128 MiB of HBM per device.

```python
import jax
import jax.numpy as jnp
from jax import lax

D = 8192
FF = 14336
SEQ_LEN = 256
ROWS = 2048
N_SECTION = 8


def draw_lengths(key, part):
    key = jax.random.fold_in(key, 11)
    first, second = jax.random.split(key)
    values = jax.random.randint(first, (N_SECTION,), SEQ_LEN // 4, SEQ_LEN + 1)
    chosen = jax.random.randint(second, (), 0, N_SECTION)
    return jnp.where(jnp.arange(N_SECTION) == chosen, SEQ_LEN, values).astype(jnp.int32)


def level_of(stream_key, shape, cuts, least, largest):
    def one(dim, parts):
        draws = jax.random.uniform(jax.random.fold_in(jax.random.fold_in(stream_key, 6), dim), (parts,), jnp.float32, least / len(cuts), largest / len(cuts))
        return jnp.repeat(jnp.exp(draws), shape[dim] // parts).reshape((-1,) + (1,) * (len(shape) - dim - 1))

    factor_of = one(*cuts[0])
    for cut in cuts[1:]:
        factor_of = factor_of * one(*cut)
    return factor_of


def bell_draw(own_key, dims, width, reach, pieces=(), kind=jnp.bfloat16):
    gain = level_of(own_key, dims, pieces, -0.22, 0.18) if pieces else 1.0
    result = jax.random.normal(own_key, dims, jnp.float32) * width * gain
    return jnp.minimum(jnp.maximum(result, -reach), reach).astype(kind)


def setup_inputs(seed: int = 0) -> dict:
    key_list = jax.random.split(jax.random.key(seed), 6)
    return {
        "states": bell_draw(key_list[0], (ROWS, D), 1.0, 6.0, ((0, 8), (1, 32))),
        "lengths": draw_lengths(jax.random.fold_in(key_list[5], 71), 0),
        "gate_weight": bell_draw(key_list[2], (D, FF), D ** -0.5, 0.0625, ((0, 256),)),
        "up_weight": bell_draw(key_list[3], (D, FF), D ** -0.5, 0.0625, ((0, 256),)),
        "upstream": bell_draw(key_list[4], (ROWS, FF), 1.0, 6.0, ((0, 8), (1, 32))),
    }


def reference(states, lengths, gate_weight, up_weight, upstream):
    hidden_parts = []
    sum_gate = jnp.zeros((D, FF), jnp.float32)
    sum_up = jnp.zeros((D, FF), jnp.float32)
    position = jnp.arange(SEQ_LEN)
    for rollout in range(N_SECTION):
        rows = states[rollout * SEQ_LEN:(rollout + 1) * SEQ_LEN]
        grads = upstream[rollout * SEQ_LEN:(rollout + 1) * SEQ_LEN].astype(jnp.float32)
        gate = jnp.dot(rows, gate_weight, preferred_element_type=jnp.float32)
        upval = jnp.dot(rows, up_weight, preferred_element_type=jnp.float32)
        sigma = jax.nn.sigmoid(gate)
        active = gate * sigma
        hidden_parts.append((active * upval).astype(jnp.bfloat16))
        live = (position < lengths[rollout])[:, None]
        grad_h = jnp.where(live, grads, 0.0)
        d_gate = (grad_h * upval * sigma * (1.0 + gate * (1.0 - sigma))).astype(jnp.bfloat16)
        d_up = (grad_h * active).astype(jnp.bfloat16)
        part_gate = jnp.dot(rows.T, d_gate, preferred_element_type=jnp.float32).astype(jnp.bfloat16)
        part_up = jnp.dot(rows.T, d_up, preferred_element_type=jnp.float32).astype(jnp.bfloat16)
        part_gate, part_up = lax.optimization_barrier((part_gate, part_up))
        sum_gate = sum_gate + part_gate.astype(jnp.float32)
        sum_up = sum_up + part_up.astype(jnp.float32)
    scale = 0.5 / jnp.sum(lengths).astype(jnp.float32)
    new_gate = (gate_weight.astype(jnp.float32) - scale * sum_gate).astype(jnp.bfloat16)
    new_up = (up_weight.astype(jnp.float32) - scale * sum_up).astype(jnp.bfloat16)
    return jnp.concatenate(hidden_parts, 0), new_gate, new_up
```

```python
import jax
import jax.numpy as jnp
from jax import lax
from jax.sharding import PartitionSpec as P


def shards(states, lengths, gate_weight, up_weight, upstream):
    sections = lax.axis_size("section")
    shard_n = lax.axis_size("shard")
    section_id = lax.axis_index("section")
    span, cols = states.shape
    quarter = shard_n // sections
    perm = []
    for s in range(sections):
        for j in range(shard_n):
            perm.append((s * shard_n + j, (j // quarter) * shard_n + s * quarter + j % quarter))
    moved = lax.ppermute(states, ("section", "shard"), perm)
    blocks = lax.all_gather(moved, "shard", axis=0, tiled=False)
    rows = blocks.reshape(sections, quarter, span, cols).transpose(0, 2, 1, 3)
    rows = rows.reshape(sections * span, quarter * cols)

    depth, units = gate_weight.shape
    width = units // shard_n
    both = jnp.concatenate(
        [gate_weight.reshape(depth, shard_n, width), up_weight.reshape(depth, shard_n, width)], 2
    )
    both = lax.all_to_all(both, "shard", split_axis=1, concat_axis=0, tiled=True)
    both = both.reshape(depth * shard_n, 2 * width)

    partial = jnp.dot(rows, both, preferred_element_type=jnp.float32).astype(jnp.bfloat16)
    pair = lax.psum_scatter(partial, "section", scatter_dimension=0, tiled=True).astype(jnp.float32)
    gate, upval = pair[:, :width], pair[:, width:]
    sigma = jax.nn.sigmoid(gate)
    active = gate * sigma
    hidden = (active * upval).astype(jnp.bfloat16)
    own_length = jnp.sum(jnp.where(jnp.arange(sections) == section_id, lengths, 0))
    live = (jnp.arange(span) < own_length)[:, None]
    grad_h = jnp.where(live, upstream.astype(jnp.float32), 0.0)
    d_gate = grad_h * upval * sigma * (1.0 + gate * (1.0 - sigma))
    d_up = grad_h * active
    stacked = jnp.concatenate([d_gate, d_up], 1).astype(jnp.bfloat16)
    grads = lax.all_gather(stacked, "section", axis=0, tiled=True)
    total = jnp.dot(rows.T, grads, preferred_element_type=jnp.float32)
    scale = 0.5 / jnp.sum(lengths).astype(jnp.float32)
    new = (both.astype(jnp.float32) - scale * total).astype(jnp.bfloat16)
    return (hidden, new[:, :width], new[:, width:])


def solution(mesh):
    in_specs = (
        P("section", "shard"),
        P(),
        P(("section", "shard"), None),
        P(("section", "shard"), None),
        P("section", "shard"),
    )
    out_specs = (P("section", "shard"), P("section", "shard"), P("section", "shard"))
    return jax.shard_map(shards, mesh=mesh, in_specs=in_specs, out_specs=out_specs, check_vma=False)
```

```python
import jax
import jax.numpy as jnp
from jax import lax
from jax.experimental import pallas as pl
from jax.experimental.pallas import tpu as pltpu
from jax.sharding import PartitionSpec as P

MESH = pl.DeviceIdType.MESH
BF16 = jnp.bfloat16
F32 = jnp.float32
NY, NX, NZ = 4, 2, 8
NSEC, NSHARD = 8, 32
ROWS = 256
DEPTH = 32
WIDTH = 448
KDIM = DEPTH * NSHARD
CHUNKS = (256, 256, 256, 128)
NC = len(CHUNKS)
OFFSETS = (0, -1, 1, -2, 2, -3, 3, 4)
STAGES = "FBXEGKH"


def kernel(lengths_ref, states_ref, gate_ref, up_ref, upstream_ref, hidden_ref, new_gate_ref, new_up_ref, *scratch):
    it = iter(scratch)
    s_buf, st_buf = next(it), next(it)
    ws, wr, p, ra, rb, qs, rx, dg = [[next(it) for _ in range(NC)] for _ in range(8)]
    (perm_s, perm_r, ring_s, ring_r, xh_s, xh_r, core_s, core_r, w_s, w_r,
     a_s, a_r, b_s, b_r, x_s, x_r, g_s, g_r) = list(it)

    sec, shard = lax.axis_index("section"), lax.axis_index("shard")
    xl, y = lax.div(sec, NY), lax.rem(sec, NY)
    z, quarter = lax.div(shard, 4), lax.rem(shard, 4)
    xh, core = lax.div(quarter, 2), lax.rem(quarter, 2)
    xo = 1 - xl
    yp, ym, yo = lax.rem(y + 1, NY), lax.rem(y + NY - 1, NY), lax.rem(y + 2, NY)
    zp, zm = lax.rem(z + 1, NZ), lax.rem(z + NZ - 1, NZ)

    def sid(x_, y_):
        return x_ * NY + y_

    def shid(z_, xh_, c_):
        return z_ * 4 + xh_ * 2 + c_

    up_dev, down_dev, xl_dev = (sid(xl, yp), shard), (sid(xl, ym), shard), (sid(xo, y), shard)
    zp_dev, zm_dev = (sec, shid(zp, xh, core)), (sec, shid(zm, xh, core))
    xh_dev, core_dev = (sec, shid(z, 1 - xh, core)), (sec, shid(z, xh, 1 - core))
    perm_dev = (z, sec * 4 + quarter)
    moves = z != sec

    barrier = pltpu.get_barrier_semaphore()

    @pl.loop(1, NSHARD)
    def _(d):
        pl.semaphore_signal(barrier, inc=1, device_id=(sec, lax.rem(shard + d, NSHARD)), device_id_type=MESH)

    for dev in (up_dev, down_dev, xl_dev):
        pl.semaphore_signal(barrier, inc=1, device_id=dev, device_id_type=MESH)

    @pl.when(moves)
    def _():
        pl.semaphore_signal(barrier, inc=1, device_id=perm_dev, device_id_type=MESH)

    pl.semaphore_wait(barrier, NSHARD - 1 + 3 + jnp.where(moves, 1, 0))

    sent = []

    def send(src, dst, ss, rs, dev):
        copy = pltpu.make_async_remote_copy(
            src_ref=src, dst_ref=dst, send_sem=ss, recv_sem=rs, device_id=dev, device_id_type=MESH
        )
        copy.start()
        sent.append((src, ss))

    def wait(ref, sem):
        pltpu.make_async_copy(ref, ref, sem).wait()

    def rows_of(section):
        return pl.ds(pl.multiple_of(section * ROWS, ROWS), ROWS)

    def cols_of(qq):
        return pl.ds(pl.multiple_of(qq * 256, 256), 256)

    own_block = s_buf.at[rows_of(z), cols_of(quarter)]
    perm_dst = s_buf.at[rows_of(sec), cols_of(quarter)]

    @pl.when(moves)
    def _():
        pltpu.make_async_remote_copy(
            src_ref=states_ref, dst_ref=perm_dst, send_sem=perm_s, recv_sem=perm_r,
            device_id=perm_dev, device_id_type=MESH,
        ).start()

    @pl.when(jnp.logical_not(moves))
    def _():
        pltpu.make_async_copy(states_ref, own_block, perm_r).start()

    lane = lax.broadcasted_iota(jnp.int32, (DEPTH, 128), 1)

    @pl.loop(0, NSHARD // 2)
    def _(m):
        both = pl.ds(pl.multiple_of(m * 2 * WIDTH, 128), 2 * WIDTH)
        g = gate_ref[:, both].astype(F32)
        u = up_ref[:, both].astype(F32)
        for odd in range(2):
            if odd:
                gv, uv = pltpu.roll(g, WIDTH, 1), pltpu.roll(u, WIDTH, 1)
                last_u = u[:, 2 * WIDTH - 128:]
            else:
                gv, uv = g, u
                last_u = pltpu.roll(u[:, 384:512], 64, 1)
            for k in range(NC - 1):
                ws[k][2 * m + odd, :, 0:128] = gv[:, k * 128:(k + 1) * 128].astype(BF16)
                ws[k][2 * m + odd, :, 128:256] = uv[:, k * 128:(k + 1) * 128].astype(BF16)
            ws[NC - 1][2 * m + odd] = jnp.where(lane < 64, gv[:, 384:512], last_u).astype(BF16)

    own_rows = pl.ds(pl.multiple_of(shard * DEPTH, DEPTH), DEPTH)

    def send_weights(k):
        @pl.loop(0, NSHARD - 1)
        def _(i):
            half = lax.div(i, 2) + 1
            d = jnp.where(lax.rem(i, 2) == 0, half, NSHARD - half)
            to = lax.rem(shard + d, NSHARD)
            pltpu.make_async_remote_copy(
                src_ref=ws[k].at[to], dst_ref=wr[k].at[own_rows], send_sem=w_s.at[k], recv_sem=w_r.at[k],
                device_id=(sec, to), device_id_type=MESH,
            ).start()

        pltpu.make_async_copy(ws[k].at[shard], wr[k].at[own_rows], w_r.at[k]).start()

    def block(off, qq):
        return s_buf.at[rows_of(lax.rem(z + off + NZ, NZ)), cols_of(qq)]

    def half_block(off, which):
        start = lax.rem(z + off + NZ, NZ) * ROWS + which * (ROWS // 2)
        return s_buf.at[pl.ds(pl.multiple_of(start, ROWS // 2), ROWS // 2), cols_of(quarter)]

    def share(i):
        ref = block(OFFSETS[i], quarter)
        send(ref, ref, xh_s.at[i], xh_r.at[i], xh_dev)
        send(ref, ref, core_s.at[0, i], core_r.at[0, i], core_dev)

    send_weights(0)
    wait(own_block, perm_r)
    send(own_block, own_block, ring_s.at[0, 0], ring_r.at[0, 0], zp_dev)
    send(own_block, own_block, ring_s.at[1, 0], ring_r.at[1, 0], zm_dev)
    share(0)
    for t in range(1, 4):
        for way in range(2):
            i = 2 * t - 1 + way
            ref = block(OFFSETS[i], quarter)
            wait(ref, ring_r.at[way, t - 1])
            onward = ref if t < 3 else half_block(OFFSETS[i], way)
            send(onward, onward, ring_s.at[way, t], ring_r.at[way, t], (zp_dev, zm_dev)[way])
            share(i)
        if t == 2:
            send_weights(1)
    for way in range(2):
        wait(half_block(4, way), ring_r.at[way, 3])
    share(7)
    send_weights(2)
    send_weights(3)
    partner = (1 - xh) * 2 + core
    for i in range(8):
        ref = block(OFFSETS[i], partner)
        wait(ref, xh_r.at[i])
        send(ref, ref, core_s.at[1, i], core_r.at[1, i], core_dev)
    for part in range(2):
        for i in range(8):
            qq = (xh if part == 0 else 1 - xh) * 2 + 1 - core
            wait(block(OFFSETS[i], qq), core_r.at[part, i])

    total = lengths_ref[0]
    for i in range(1, NSEC):
        total = total + lengths_ref[i]
    own_length = lengths_ref[sec]
    live = lax.broadcasted_iota(jnp.int32, (ROWS, 128), 0) < own_length

    def forward(k, section):
        r = rows_of(section)
        p[k][r, :] = jnp.dot(s_buf[r, :], wr[k][...], preferred_element_type=F32).astype(BF16)

    def stage_f(k):
        wait(wr[k], w_r.at[k])

        @pl.loop(0, 2)
        def _(i):
            forward(k, sid(i, yo))

        def part(x_, y_):
            return p[k].at[rows_of(sid(x_, y_))]

        send(part(0, yo), ra[k].at[0], a_s.at[k, 0], a_r.at[k, 0], up_dev)
        send(part(1, yo), ra[k].at[1], a_s.at[k, 1], a_r.at[k, 1], down_dev)

        @pl.loop(0, 4)
        def _(i):
            forward(k, sid(lax.rem(i, 2), jnp.where(i < 2, yp, ym)))

        send(part(1, yp), rb[k].at[1], b_s.at[k, 1], b_r.at[k, 1], up_dev)
        send(part(0, ym), rb[k].at[2], b_s.at[k, 2], b_r.at[k, 2], down_dev)

        @pl.loop(0, 2)
        def _(i):
            forward(k, sid(i, y))

    def stage_b(k):
        for way in range(2):
            wait(ra[k].at[way], a_r.at[k, way])
            r = rows_of(sid(way, (yp, ym)[way]))
            p[k][r, :] = (p[k][r, :].astype(F32) + ra[k][way].astype(F32)).astype(BF16)
            slot = (0, 3)[way]
            send(p[k].at[r], rb[k].at[slot], b_s.at[k, slot], b_r.at[k, slot], (up_dev, down_dev)[way])

    def stage_x(k):
        for slot in range(4):
            wait(rb[k].at[slot], b_r.at[k, slot])

        def summed(x_):
            r = rows_of(sid(x_, y))
            return p[k][r, :].astype(F32) + rb[k][x_].astype(F32) + rb[k][2 + x_].astype(F32)

        other = rows_of(sid(xo, y))
        p[k][other, :] = summed(xo).astype(BF16)
        send(p[k].at[other], rx[k], x_s.at[k], x_r.at[k], xl_dev)
        qs[k][...] = summed(xl)

    own_r = rows_of(sec)

    def grads(gate, upval, upstream, alive):
        sigma = 1.0 / (1.0 + jnp.exp(-gate))
        active = gate * sigma
        hid = (active * upval).astype(BF16)
        dh = jnp.where(alive, upstream.astype(F32), 0.0)
        d_gate = dh * upval * sigma * (1.0 + gate * (1.0 - sigma))
        return hid, d_gate, dh * active

    def stage_e(k):
        wait(rx[k], x_r.at[k])
        val = qs[k][...] + rx[k][...].astype(F32)
        if k < NC - 1:
            cols = slice(k * 128, (k + 1) * 128)
            hid, d_gate, d_up = grads(val[:, :128], val[:, 128:], upstream_ref[:, cols], live)
            hidden_ref[:, cols] = hid
            dg[k][own_r, 0:128] = d_gate.astype(BF16)
            dg[k][own_r, 128:256] = d_up.astype(BF16)
        else:
            cols = slice(k * 128, k * 128 + 64)
            hid, d_gate, d_up = grads(
                val[:, :64], pltpu.roll(val, 64, 1)[:, :64], upstream_ref[:, cols], live[:, :64]
            )
            hidden_ref[:, cols] = hid
            dg[k][own_r, :] = jnp.concatenate([d_gate, d_up], 1).astype(BF16)
        ref = dg[k].at[own_r]
        for slot, dev in ((0, xl_dev), (1, up_dev), (2, down_dev)):
            send(ref, ref, g_s.at[k, slot], g_r.at[k, slot], dev)

    def grad_block(k, x_, y_):
        return dg[k].at[rows_of(sid(x_, y_))]

    def stage_g(k):
        ref = grad_block(k, xo, y)
        wait(ref, g_r.at[k, 0])
        send(ref, ref, g_s.at[k, 3], g_r.at[k, 3], up_dev)
        send(ref, ref, g_s.at[k, 4], g_r.at[k, 4], down_dev)

    def stage_k(k):
        ref = grad_block(k, xl, ym)
        wait(ref, g_r.at[k, 1])
        send(ref, ref, g_s.at[k, 5], g_r.at[k, 5], up_dev)
        ref = grad_block(k, xo, yp)
        wait(ref, g_r.at[k, 4])
        send(ref, ref, g_s.at[k, 6], g_r.at[k, 6], down_dev)

    scale = 0.5 / jnp.full((ROWS, 128), total.astype(F32), F32)

    def stage_h(k):
        wait(grad_block(k, xl, yp), g_r.at[k, 2])
        wait(grad_block(k, xo, ym), g_r.at[k, 3])
        wait(grad_block(k, xl, yo), g_r.at[k, 5])
        wait(grad_block(k, xo, yo), g_r.at[k, 6])

        @pl.loop(0, KDIM // ROWS)
        def _(i):
            r = rows_of(i)
            acc = jnp.dot(st_buf[r, :], dg[k][...], preferred_element_type=F32)
            old = wr[k][r, :].astype(F32)
            first = old[:, :128] - scale * acc[:, :128]
            if k < NC - 1:
                cols = slice(k * 128, (k + 1) * 128)
                new_gate_ref[r, cols] = first.astype(BF16)
                new_up_ref[r, cols] = (old[:, 128:] - scale * acc[:, 128:]).astype(BF16)
            else:
                cols = slice(k * 128, k * 128 + 64)
                new_gate_ref[r, cols] = first[:, :64].astype(BF16)
                new_up_ref[r, cols] = pltpu.roll(first, 64, 1)[:, :64].astype(BF16)

    run = {"F": stage_f, "B": stage_b, "X": stage_x, "E": stage_e, "G": stage_g, "K": stage_k, "H": stage_h}
    order = sorted((2 * k + n, -n, name, k) for k in range(NC) for n, name in enumerate(STAGES))
    for _, _, name, k in order:
        run[name](k)
        if name == "F" and k == 0:
            @pl.loop(0, NSEC)
            def _(i):
                r = rows_of(i)
                st_buf[:, r] = s_buf[r, :].T

    @pl.when(moves)
    def _():
        wait(states_ref, perm_s)

    for k in range(NC):
        gone = ws[k].at[pl.ds(0, NSHARD - 1)]
        wait(gone, w_s.at[k])
    for src, ss in sent:
        wait(src, ss)


def shards(states, lengths, gate_weight, up_weight, upstream):
    vmem = pl.BlockSpec(memory_space=pltpu.VMEM)
    dma = pltpu.SemaphoreType.DMA
    buffers = [pltpu.VMEM((NSEC * ROWS, KDIM), BF16), pltpu.VMEM((KDIM, NSEC * ROWS), BF16)]
    for shape, kind in (
        ((NSHARD, DEPTH), BF16), ((KDIM,), BF16), ((NSEC * ROWS,), BF16), ((2, ROWS), BF16), ((4, ROWS), BF16),
        ((ROWS,), F32), ((ROWS,), BF16), ((NSEC * ROWS,), BF16),
    ):
        buffers += [pltpu.VMEM(shape + (n,), kind) for n in CHUNKS]
    sems = [dma, dma, dma((2, 4)), dma((2, 4)), dma((8,)), dma((8,)), dma((2, 8)), dma((2, 8)), dma((NC,)), dma((NC,)),
            dma((NC, 2)), dma((NC, 2)), dma((NC, 4)), dma((NC, 4)), dma((NC,)), dma((NC,)), dma((NC, 7)), dma((NC, 7))]
    return pl.pallas_call(
        kernel,
        out_shape=(
            jax.ShapeDtypeStruct((ROWS, WIDTH), BF16),
            jax.ShapeDtypeStruct((KDIM, WIDTH), BF16),
            jax.ShapeDtypeStruct((KDIM, WIDTH), BF16),
        ),
        in_specs=[pl.BlockSpec(memory_space=pltpu.SMEM)] + [vmem] * 4,
        out_specs=(vmem, vmem, vmem),
        scratch_shapes=buffers + sems,
        compiler_params=pltpu.CompilerParams(collective_id=0, has_side_effects=True, vmem_limit_bytes=56 << 20),
        cost_estimate=pl.CostEstimate(flops=7516192768, bytes_accessed=8 << 20, transcendentals=ROWS * WIDTH),
        name="projection_pair",
    )(lengths, states, gate_weight, up_weight, upstream)


def solution(mesh):
    in_specs = (
        P("section", "shard"),
        P(),
        P(("section", "shard"), None),
        P(("section", "shard"), None),
        P("section", "shard"),
    )
    out_specs = (P("section", "shard"), P("section", "shard"), P("section", "shard"))
    return jax.shard_map(shards, mesh=mesh, in_specs=in_specs, out_specs=out_specs, check_vma=False)
```

```python
import jax
import jax.numpy as jnp
from jax import lax
from jax.experimental import pallas as pl
from jax.experimental.pallas import tpu as pltpu
from jax.sharding import PartitionSpec as P

MESH = pl.DeviceIdType.MESH
BF16 = jnp.bfloat16
F32 = jnp.float32
NY, NX, NZ = 4, 2, 8
NSEC, NSHARD = 8, 32
ROWS = 256
DEPTH = 32
WIDTH = 448
KDIM = DEPTH * NSHARD
UNITS = 64
TILES = (1, 1, 1, 1, 1, 1, 1)
NC = len(TILES)
FIRST = tuple(sum(TILES[:k]) for k in range(NC))
AHEAD = 2
LAG = 2
OFFSETS = (0, -1, 1, -2, 2, -3, 3, 4)
STAGES = "FBXEGKH"


def kernel(lengths_ref, states_hbm, gate_hbm, up_hbm, upstream_hbm, hidden_hbm, new_gate_hbm, new_up_hbm, *scratch):
    it = iter(scratch)
    gate_ref, up_ref, upstream_ref, hidden_ref, new_gate_ref, new_up_ref, stage, s_buf = [next(it) for _ in range(8)]
    ws, wr, wt, p, ra, rb, qs, rx, dg = [[next(it) for _ in range(NC)] for _ in range(9)]
    (in_s, out_s, ring_s, ring_r, sec_s, sec_r, core_s, core_r, w_s, w_r,
     a_s, a_r, b_s, b_r, x_s, x_r, g_s, g_r) = list(it)

    sec, shard = lax.axis_index("section"), lax.axis_index("shard")
    xl, y = lax.div(sec, NY), lax.rem(sec, NY)
    z, quarter = lax.div(shard, 4), lax.rem(shard, 4)
    xh, core = lax.div(quarter, 2), lax.rem(quarter, 2)
    xo = 1 - xl
    yp, ym, yo = lax.rem(y + 1, NY), lax.rem(y + NY - 1, NY), lax.rem(y + 2, NY)
    zp, zm = lax.rem(z + 1, NZ), lax.rem(z + NZ - 1, NZ)

    def sid(x_, y_):
        return x_ * NY + y_

    def shid(z_, xh_, c_):
        return z_ * 4 + xh_ * 2 + c_

    up_dev, down_dev, xl_dev = (sid(xl, yp), shard), (sid(xl, ym), shard), (sid(xo, y), shard)
    zp_dev, zm_dev = (sec, shid(zp, xh, core)), (sec, shid(zm, xh, core))
    core_dev = (sec, shid(z, xh, 1 - core))

    barrier = pltpu.get_barrier_semaphore()

    @pl.loop(1, NSEC)
    def _(d):
        to = lax.rem(sec + d, NSEC)
        pl.semaphore_signal(barrier, inc=1, device_id=(to, shard), device_id_type=MESH)
        pl.semaphore_signal(barrier, inc=1, device_id=(to, shid(z, 1 - xh, core)), device_id_type=MESH)

    @pl.loop(1, NSHARD)
    def _(d):
        pl.semaphore_signal(barrier, inc=1, device_id=(sec, lax.rem(shard + d, NSHARD)), device_id_type=MESH)

    loads = [
        pltpu.make_async_copy(src, dst, in_s.at[i])
        for i, (src, dst) in enumerate((
            (states_hbm, stage.at[z]), (gate_hbm, gate_ref), (up_hbm, up_ref), (upstream_hbm, upstream_ref),
        ))
    ]
    for copy in loads:
        copy.start()

    sent = []

    def send(src, dst, ss, rs, dev):
        pltpu.make_async_remote_copy(
            src_ref=src, dst_ref=dst, send_sem=ss, recv_sem=rs, device_id=dev, device_id_type=MESH
        ).start()
        sent.append((src, ss))

    def wait(ref, sem):
        pltpu.make_async_copy(ref, ref, sem).wait()

    def rows_of(section):
        return pl.ds(pl.multiple_of(section * ROWS, ROWS), ROWS)

    def cols_of(qq):
        return pl.ds(pl.multiple_of(qq * 256, 256), 256)

    lane = lax.broadcasted_iota(jnp.int32, (DEPTH, 128), 1)
    loads[1].wait()
    loads[2].wait()

    @pl.loop(0, NSHARD // 2)
    def _(m):
        for k in range(NC):
            for t in range(TILES[k]):
                for odd in range(2):
                    a = odd * (WIDTH // UNITS) + FIRST[k] + t
                    cols = pl.ds(pl.multiple_of(m * 2 * WIDTH + (a // 2) * 128, 128), 128)
                    g, u = gate_ref[:, cols].astype(F32), up_ref[:, cols].astype(F32)
                    if a % 2:
                        val = jnp.where(lane < UNITS, pltpu.roll(g, UNITS, 1), u)
                    else:
                        val = jnp.where(lane < UNITS, g, pltpu.roll(u, UNITS, 1))
                    ws[k][2 * m + odd, :, t * 128:(t + 1) * 128] = val.astype(BF16)

    own_rows = pl.ds(pl.multiple_of(shard * DEPTH, DEPTH), DEPTH)

    def send_weights(k):
        @pl.loop(0, NSHARD - 1)
        def _(i):
            half = lax.div(i, 2) + 1
            d = jnp.where(lax.rem(i, 2) == 0, half, NSHARD - half)
            to = lax.rem(shard + d, NSHARD)
            pltpu.make_async_remote_copy(
                src_ref=ws[k].at[to], dst_ref=wr[k].at[own_rows], send_sem=w_s.at[k], recv_sem=w_r.at[k],
                device_id=(sec, to), device_id_type=MESH,
            ).start()

        pltpu.make_async_copy(ws[k].at[shard], wr[k].at[own_rows], w_r.at[k]).start()

    loads[0].wait()
    pl.semaphore_wait(barrier, NSHARD - 1 + 2 * (NSEC - 1))

    def zed(off):
        return lax.rem(z + off + NZ, NZ)

    def half_block(off, which):
        return stage.at[zed(off), pl.ds(which * (ROWS // 2), ROWS // 2)]

    own_slot = s_buf.at[rows_of(sec), cols_of(quarter)]

    def dispatch(i):
        k = zed(OFFSETS[i])
        src = stage.at[k]

        @pl.when(k != sec)
        def _():
            pltpu.make_async_remote_copy(
                src_ref=src, dst_ref=own_slot, send_sem=sec_s.at[i, 0], recv_sem=sec_r.at[sec, xh],
                device_id=(k, shard), device_id_type=MESH,
            ).start()

        @pl.when(k == sec)
        def _():
            pltpu.make_async_copy(src, own_slot, sec_r.at[sec, xh]).start()

        send(src, own_slot, sec_s.at[i, 1], sec_r.at[sec, xh], (k, shid(z, 1 - xh, core)))

    send(stage.at[z], stage.at[z], ring_s.at[0, 0], ring_r.at[0, 0], zp_dev)
    send(stage.at[z], stage.at[z], ring_s.at[1, 0], ring_r.at[1, 0], zm_dev)
    dispatch(0)
    send_weights(0)
    for t in range(1, 4):
        for way in range(2):
            i = 2 * t - 1 + way
            ref = stage.at[zed(OFFSETS[i])]
            wait(ref, ring_r.at[way, t - 1])
            onward = ref if t < 3 else half_block(OFFSETS[i], way)
            send(onward, onward, ring_s.at[way, t], ring_r.at[way, t], (zp_dev, zm_dev)[way])
            dispatch(i)
    for way in range(2):
        wait(half_block(4, way), ring_r.at[way, 3])
    dispatch(7)
    for k in range(1, AHEAD):
        send_weights(k)

    @pl.loop(0, NSEC)
    def _(d):
        s = lax.rem(sec + d, NSEC)
        for x_ in range(2):
            ref = s_buf.at[rows_of(s), cols_of(x_ * 2 + core)]
            wait(ref, sec_r.at[s, x_])
            pltpu.make_async_remote_copy(
                src_ref=ref, dst_ref=ref, send_sem=core_s.at[s, x_], recv_sem=core_r.at[s, x_],
                device_id=core_dev, device_id_type=MESH,
            ).start()

    @pl.loop(0, NSEC)
    def _(s):
        for x_ in range(2):
            wait(s_buf.at[rows_of(s), cols_of(x_ * 2 + 1 - core)], core_r.at[s, x_])

    loads[3].wait()
    total = lengths_ref[0]
    for i in range(1, NSEC):
        total = total + lengths_ref[i]
    live = lax.broadcasted_iota(jnp.int32, (UNITS, ROWS), 1) < lengths_ref[sec]
    scale = 0.5 / jnp.full((UNITS, 256), total.astype(F32), F32)

    def forward(k, section):
        acc = lax.dot_general(
            wt[k][...], s_buf[rows_of(section), :], (((1,), (1,)), ((), ())), preferred_element_type=F32
        )
        p[k][section] = acc.astype(BF16)

    def stage_f(k):
        wait(wr[k], w_r.at[k])
        if k + AHEAD < NC:
            send_weights(k + AHEAD)

        @pl.loop(0, KDIM // 256)
        def _(i):
            wt[k][:, cols_of(i)] = wr[k][cols_of(i), :].T

        @pl.loop(0, 2)
        def _(i):
            forward(k, sid(i, yo))

        send(p[k].at[sid(0, yo)], ra[k].at[0], a_s.at[k, 0], a_r.at[k, 0], up_dev)
        send(p[k].at[sid(1, yo)], ra[k].at[1], a_s.at[k, 1], a_r.at[k, 1], down_dev)

        @pl.loop(0, 4)
        def _(i):
            forward(k, sid(lax.rem(i, 2), jnp.where(i < 2, yp, ym)))

        send(p[k].at[sid(1, yp)], rb[k].at[1], b_s.at[k, 1], b_r.at[k, 1], up_dev)
        send(p[k].at[sid(0, ym)], rb[k].at[2], b_s.at[k, 2], b_r.at[k, 2], down_dev)

        @pl.loop(0, 2)
        def _(i):
            forward(k, sid(i, y))

    def stage_b(k):
        for way in range(2):
            wait(ra[k].at[way], a_r.at[k, way])
            s = sid(way, (yp, ym)[way])
            p[k][s] = (p[k][s].astype(F32) + ra[k][way].astype(F32)).astype(BF16)
            slot = (0, 3)[way]
            send(p[k].at[s], rb[k].at[slot], b_s.at[k, slot], b_r.at[k, slot], (up_dev, down_dev)[way])

    def stage_x(k):
        for slot in range(4):
            wait(rb[k].at[slot], b_r.at[k, slot])

        def summed(x_):
            return p[k][sid(x_, y)].astype(F32) + rb[k][x_].astype(F32) + rb[k][2 + x_].astype(F32)

        other = sid(xo, y)
        p[k][other] = summed(xo).astype(BF16)
        send(p[k].at[other], rx[k], x_s.at[k], x_r.at[k], xl_dev)
        qs[k][...] = summed(xl)

    def grad_block(k, x_, y_):
        return dg[k].at[:, rows_of(sid(x_, y_))]

    def stage_e(k):
        wait(rx[k], x_r.at[k])
        for t in range(TILES[k]):
            low, high = slice(t * 128, t * 128 + UNITS), slice(t * 128 + UNITS, (t + 1) * 128)
            units = slice((FIRST[k] + t) * UNITS, (FIRST[k] + t + 1) * UNITS)
            gate = qs[k][low] + rx[k][low].astype(F32)
            upval = qs[k][high] + rx[k][high].astype(F32)
            sigma = 1.0 / (1.0 + jnp.exp(-gate))
            active = gate * sigma
            hidden_ref[units] = (active * upval).astype(BF16)
            dh = jnp.where(live, upstream_ref[units].astype(F32), 0.0)
            d_gate = dh * upval * sigma * (1.0 + gate * (1.0 - sigma))
            dg[k][low, rows_of(sec)] = d_gate.astype(BF16)
            dg[k][high, rows_of(sec)] = (dh * active).astype(BF16)
        ref = grad_block(k, xl, y)
        for slot, dev in ((0, xl_dev), (1, up_dev), (2, down_dev)):
            send(ref, ref, g_s.at[k, slot], g_r.at[k, slot], dev)

    def stage_g(k):
        ref = grad_block(k, xo, y)
        wait(ref, g_r.at[k, 0])
        send(ref, ref, g_s.at[k, 3], g_r.at[k, 3], up_dev)
        send(ref, ref, g_s.at[k, 4], g_r.at[k, 4], down_dev)

    def stage_k(k):
        ref = grad_block(k, xl, ym)
        wait(ref, g_r.at[k, 1])
        send(ref, ref, g_s.at[k, 5], g_r.at[k, 5], up_dev)
        ref = grad_block(k, xo, yp)
        wait(ref, g_r.at[k, 4])
        send(ref, ref, g_s.at[k, 6], g_r.at[k, 6], down_dev)

    stores = []

    def stage_h(k):
        wait(grad_block(k, xl, yp), g_r.at[k, 2])
        wait(grad_block(k, xo, ym), g_r.at[k, 3])
        wait(grad_block(k, xl, yo), g_r.at[k, 5])
        wait(grad_block(k, xo, yo), g_r.at[k, 6])

        @pl.loop(0, KDIM // 256)
        def _(i):
            cols = cols_of(i)
            acc = jnp.dot(dg[k][...], s_buf[:, cols], preferred_element_type=F32)
            for t in range(TILES[k]):
                low, high = slice(t * 128, t * 128 + UNITS), slice(t * 128 + UNITS, (t + 1) * 128)
                units = slice((FIRST[k] + t) * UNITS, (FIRST[k] + t + 1) * UNITS)
                new_gate_ref[units, cols] = (wt[k][low, cols].astype(F32) - scale * acc[low]).astype(BF16)
                new_up_ref[units, cols] = (wt[k][high, cols].astype(F32) - scale * acc[high]).astype(BF16)

        part = pl.ds(FIRST[k] * UNITS, TILES[k] * UNITS)
        for n, (src, dst) in enumerate(((hidden_ref, hidden_hbm), (new_gate_ref, new_gate_hbm), (new_up_ref, new_up_hbm))):
            copy = pltpu.make_async_copy(src.at[part], dst.at[part], out_s.at[k, n])
            copy.start()
            stores.append(copy)

    run = {"F": stage_f, "B": stage_b, "X": stage_x, "E": stage_e, "G": stage_g, "K": stage_k, "H": stage_h}
    order = sorted((LAG * k + n, -n, name, k) for k in range(NC) for n, name in enumerate(STAGES))
    for _, _, name, k in order:
        run[name](k)

    for i in range(NZ):
        @pl.when(zed(OFFSETS[i]) != sec)
        def _():
            wait(stage.at[0], sec_s.at[i, 0])

    @pl.loop(0, NSEC)
    def _(s):
        for x_ in range(2):
            wait(stage.at[0], core_s.at[s, x_])

    for k in range(NC):
        wait(ws[k].at[pl.ds(0, NSHARD - 1)], w_s.at[k])
    for src, ss in sent:
        wait(src, ss)
    for copy in stores:
        copy.wait()


def shards(states, lengths, gate_weight, up_weight, upstream):
    hbm = pl.BlockSpec(memory_space=pl.ANY)
    dma = pltpu.SemaphoreType.DMA
    buffers = [
        pltpu.VMEM(shape, BF16)
        for shape in (
            (DEPTH, WIDTH * NSHARD), (DEPTH, WIDTH * NSHARD), (WIDTH, ROWS), (WIDTH, ROWS), (WIDTH, KDIM), (WIDTH, KDIM),
            (NZ, ROWS, 256), (NSEC * ROWS, KDIM),
        )
    ]
    sizes = [128 * t for t in TILES]
    for shape, kind in (
        (lambda n: (NSHARD, DEPTH, n), BF16), (lambda n: (KDIM, n), BF16), (lambda n: (n, KDIM), BF16),
        (lambda n: (NSEC, n, ROWS), BF16), (lambda n: (2, n, ROWS), BF16), (lambda n: (4, n, ROWS), BF16),
        (lambda n: (n, ROWS), F32), (lambda n: (n, ROWS), BF16), (lambda n: (n, NSEC * ROWS), BF16),
    ):
        buffers += [pltpu.VMEM(shape(n), kind) for n in sizes]
    sems = [dma((4,)), dma((NC, 3)), dma((2, 4)), dma((2, 4)), dma((NZ, 2)), dma((NSEC, 2)), dma((NSEC, 2)), dma((NSEC, 2)),
            dma((NC,)), dma((NC,)), dma((NC, 2)), dma((NC, 2)), dma((NC, 4)), dma((NC, 4)), dma((NC,)), dma((NC,)),
            dma((NC, 7)), dma((NC, 7))]
    hidden, new_gate, new_up = pl.pallas_call(
        kernel,
        out_shape=(
            jax.ShapeDtypeStruct((WIDTH, ROWS), BF16),
            jax.ShapeDtypeStruct((WIDTH, KDIM), BF16),
            jax.ShapeDtypeStruct((WIDTH, KDIM), BF16),
        ),
        in_specs=[pl.BlockSpec(memory_space=pltpu.SMEM)] + [hbm] * 4,
        out_specs=(hbm, hbm, hbm),
        scratch_shapes=buffers + sems,
        compiler_params=pltpu.CompilerParams(collective_id=0, has_side_effects=True, vmem_limit_bytes=56 << 20),
        cost_estimate=pl.CostEstimate(flops=7516192768, bytes_accessed=8 << 20, transcendentals=ROWS * WIDTH),
        name="projection_pair",
    )(lengths, states, gate_weight, up_weight, upstream.T)
    return hidden.T, new_gate.T, new_up.T


def solution(mesh):
    in_specs = (
        P("section", "shard"),
        P(),
        P(("section", "shard"), None),
        P(("section", "shard"), None),
        P("section", "shard"),
    )
    out_specs = (P("section", "shard"), P("section", "shard"), P("section", "shard"))
    return jax.shard_map(shards, mesh=mesh, in_specs=in_specs, out_specs=out_specs, check_vma=False)
```

```python
import jax
import jax.numpy as jnp
from jax import lax
from jax.experimental import pallas as pl
from jax.experimental.pallas import tpu as pltpu
from jax.sharding import PartitionSpec as P

MESH = pl.DeviceIdType.MESH
BF16 = jnp.bfloat16
F32 = jnp.float32
NY, NX, NZ = 4, 2, 8
NSEC, NSHARD = 8, 32
ROWS = 256
DEPTH = 32
WIDTH = 448
KDIM = DEPTH * NSHARD
UNITS = 64
TILES = (1, 2, 2, 2)
NC = len(TILES)
FIRST = tuple(sum(TILES[:k]) for k in range(NC))
AHEAD = 2
LAG = 1
OFFSETS = (0, -1, 1, -2, 2, -3, 3, 4)
STAGES = "FBXEGKH"


def kernel(lengths_ref, states_ref, gate_ref, up_ref, upstream_ref, hidden_ref, new_gate_ref, new_up_ref, *scratch):
    it = iter(scratch)
    mid, s_buf, st_buf, acc = [next(it) for _ in range(4)]
    ws, wr, wt, p, ra, rb, qs, rx, dg = [[next(it) for _ in range(NC)] for _ in range(9)]
    (mid_s, mid_r, ring_s, ring_r, far_s, far_r, xh_s, xh_r, core_s, core_r, w_s, w_r,
     a_s, a_r, b_s, b_r, x_s, x_r, g_s, g_r) = list(it)

    sec, shard = lax.axis_index("section"), lax.axis_index("shard")
    xl, y = lax.div(sec, NY), lax.rem(sec, NY)
    z, quarter = lax.div(shard, 4), lax.rem(shard, 4)
    xh, core = lax.div(quarter, 2), lax.rem(quarter, 2)
    xo = 1 - xl
    yp, ym, yo = lax.rem(y + 1, NY), lax.rem(y + NY - 1, NY), lax.rem(y + 2, NY)
    zp, zm = lax.rem(z + 1, NZ), lax.rem(z + NZ - 1, NZ)

    def sid(x_, y_):
        return x_ * NY + y_

    def shid(z_, xh_, c_):
        return z_ * 4 + xh_ * 2 + c_

    up_dev, down_dev, xl_dev = (sid(xl, yp), shard), (sid(xl, ym), shard), (sid(xo, y), shard)
    zp_dev, zm_dev = (sec, shid(zp, xh, core)), (sec, shid(zm, xh, core))
    core_dev, xh_dev = (sec, shid(z, xh, 1 - core)), (sec, shid(z, 1 - xh, core))
    mid_dev, goal = (sec, shid(lax.rem(z + sec, NZ), xh, core)), lax.rem(z - sec + NZ, NZ)

    barrier = pltpu.get_barrier_semaphore()

    @pl.loop(1, NSEC)
    def _(d):
        to = lax.rem(sec + d, NSEC)
        pl.semaphore_signal(barrier, inc=1, device_id=(to, shard), device_id_type=MESH)

    @pl.loop(1, NSHARD)
    def _(d):
        pl.semaphore_signal(barrier, inc=1, device_id=(sec, lax.rem(shard + d, NSHARD)), device_id_type=MESH)

    sent = []

    def send(src, dst, ss, rs, dev):
        pltpu.make_async_remote_copy(
            src_ref=src, dst_ref=dst, send_sem=ss, recv_sem=rs, device_id=dev, device_id_type=MESH
        ).start()
        sent.append((src, ss))

    def wait(ref, sem):
        pltpu.make_async_copy(ref, ref, sem).wait()

    def slot_of(section):
        return lax.rem(section, NY) * NX + lax.div(section, NY)

    def rows_of(section):
        return pl.ds(pl.multiple_of(slot_of(section) * ROWS, ROWS), ROWS)

    def pair_of(y_):
        return pl.ds(pl.multiple_of(y_ * NX * ROWS, NX * ROWS), NX * ROWS)

    def cols_of(qq):
        return pl.ds(pl.multiple_of(qq * 256, 256), 256)

    lane = lax.broadcasted_iota(jnp.int32, (DEPTH, 128), 1)

    @pl.loop(0, NSHARD // 2)
    def _(m):
        for k in range(NC):
            for t in range(TILES[k]):
                for odd in range(2):
                    a = odd * (WIDTH // UNITS) + FIRST[k] + t
                    cols = pl.ds(pl.multiple_of(m * 2 * WIDTH + (a // 2) * 128, 128), 128)
                    g, u = gate_ref[:, cols].astype(F32), up_ref[:, cols].astype(F32)
                    if a % 2:
                        val = jnp.where(lane < UNITS, pltpu.roll(g, UNITS, 1), u)
                    else:
                        val = jnp.where(lane < UNITS, g, pltpu.roll(u, UNITS, 1))
                    ws[k][2 * m + odd, :, t * 128:(t + 1) * 128] = val.astype(BF16)

    own_rows = pl.ds(pl.multiple_of(shard * DEPTH, DEPTH), DEPTH)

    def send_weights(k):
        @pl.loop(0, NSHARD - 1)
        def _(i):
            half = lax.div(i, 2) + 1
            d = jnp.where(lax.rem(i, 2) == 0, half, NSHARD - half)
            to = lax.rem(shard + d, NSHARD)
            pltpu.make_async_remote_copy(
                src_ref=ws[k].at[to], dst_ref=wr[k].at[own_rows], send_sem=w_s.at[k], recv_sem=w_r.at[k],
                device_id=(sec, to), device_id_type=MESH,
            ).start()

        pltpu.make_async_copy(ws[k].at[shard], wr[k].at[own_rows], w_r.at[k]).start()

    pl.semaphore_wait(barrier, NSHARD - 1 + NSEC - 1)

    @pl.when(sec != 0)
    def _():
        pltpu.make_async_remote_copy(
            src_ref=states_ref, dst_ref=mid, send_sem=mid_s.at[0], recv_sem=mid_r.at[0],
            device_id=mid_dev, device_id_type=MESH,
        ).start()

    @pl.when(sec == 0)
    def _():
        pltpu.make_async_copy(states_ref, mid, mid_r.at[0]).start()

    def block(off, qq):
        return s_buf.at[rows_of(lax.rem(goal + off + NZ, NZ)), cols_of(qq)]

    def half_block(off, which, qq):
        start = slot_of(lax.rem(goal + off + NZ, NZ)) * ROWS + which * (ROWS // 2)
        return s_buf.at[pl.ds(pl.multiple_of(start, ROWS // 2), ROWS // 2), cols_of(qq)]

    partner = (1 - xh) * 2 + core
    z_devs = (zp_dev, zm_dev)

    def share(i, part):
        ref = block(OFFSETS[i], (quarter, partner)[part])
        if part == 0 and i < 5:
            send(ref, ref, xh_s.at[i], xh_r.at[i], xh_dev)
        send(ref, ref, core_s.at[part, i], core_r.at[part, i], core_dev)

    def onward(i, way, half, qq, ss, rs):
        ref = half_block(OFFSETS[i], way, qq) if half else block(OFFSETS[i], qq)
        send(ref, ref, ss, rs, z_devs[way])

    send_weights(0)
    wait(mid, mid_r.at[0])
    to_rows = s_buf.at[rows_of(sec), cols_of(quarter)]

    @pl.when(goal != sec)
    def _():
        pltpu.make_async_remote_copy(
            src_ref=mid, dst_ref=to_rows, send_sem=mid_s.at[1], recv_sem=mid_r.at[1],
            device_id=(goal, shard), device_id_type=MESH,
        ).start()

    @pl.when(goal == sec)
    def _():
        pltpu.make_async_copy(mid, to_rows, mid_r.at[1]).start()

    wait(block(0, quarter), mid_r.at[1])
    for way in range(2):
        onward(0, way, False, quarter, ring_s.at[way, 0], ring_r.at[way, 0])
    share(0, 0)
    for t in range(1, 4):
        for way in range(2):
            i = 2 * t - 1 + way
            wait(block(OFFSETS[i], quarter), ring_r.at[way, t - 1])
            onward(i, way, t == 3, quarter, ring_s.at[way, t], ring_r.at[way, t])
            share(i, 0)
    for i in range(5):
        wait(block(OFFSETS[i], partner), xh_r.at[i])
        if i > 2:
            onward(i, i - 3, False, partner, far_s.at[i - 3, 0], far_r.at[i - 3, 0])
        share(i, 1)
    for way in range(2):
        wait(half_block(4, way, quarter), ring_r.at[way, 3])
    share(7, 0)
    for way in range(2):
        wait(block(OFFSETS[5 + way], partner), far_r.at[way, 0])
        onward(5 + way, way, True, partner, far_s.at[way, 1], far_r.at[way, 1])
        share(5 + way, 1)
    for k in range(1, AHEAD):
        send_weights(k)
    for way in range(2):
        wait(half_block(4, way, partner), far_r.at[way, 1])
    share(7, 1)
    for part in range(2):
        for i in range(8):
            wait(block(OFFSETS[i], (quarter, partner)[part] + 1 - 2 * core), core_r.at[part, i])

    total = lengths_ref[0]
    for i in range(1, NSEC):
        total = total + lengths_ref[i]
    live = lax.broadcasted_iota(jnp.int32, (UNITS, ROWS), 1) < lengths_ref[sec]
    scale = 0.5 / jnp.full((UNITS, 256), total.astype(F32), F32)

    def forward(k, y_):
        p[k][pair_of(y_), :] = jnp.dot(s_buf[pair_of(y_), :], wr[k][...], preferred_element_type=F32).astype(BF16)

    def part(k, x_, y_):
        return p[k].at[rows_of(sid(x_, y_))]

    def stage_f(k):
        wait(wr[k], w_r.at[k])
        if k + AHEAD < NC:
            send_weights(k + AHEAD)

        forward(k, yo)
        send(part(k, 0, yo), ra[k].at[0], a_s.at[k, 0], a_r.at[k, 0], up_dev)
        send(part(k, 1, yo), ra[k].at[1], a_s.at[k, 1], a_r.at[k, 1], down_dev)
        forward(k, yp)
        send(part(k, 1, yp), rb[k].at[1], b_s.at[k, 1], b_r.at[k, 1], up_dev)
        forward(k, ym)
        send(part(k, 0, ym), rb[k].at[2], b_s.at[k, 2], b_r.at[k, 2], down_dev)
        forward(k, y)

        @pl.loop(0, KDIM // 256)
        def _(i):
            wt[k][:, cols_of(i)] = wr[k][cols_of(i), :].T

    def stage_b(k):
        for way in range(2):
            wait(ra[k].at[way], a_r.at[k, way])
            r = rows_of(sid(way, (yp, ym)[way]))
            p[k][r, :] = (p[k][r, :].astype(F32) + ra[k][way].astype(F32)).astype(BF16)
            slot = (0, 3)[way]
            send(p[k].at[r], rb[k].at[slot], b_s.at[k, slot], b_r.at[k, slot], (up_dev, down_dev)[way])

    def stage_x(k):
        for slot in range(4):
            wait(rb[k].at[slot], b_r.at[k, slot])

        def summed(x_):
            r = rows_of(sid(x_, y))
            return p[k][r, :].astype(F32) + rb[k][x_].astype(F32) + rb[k][2 + x_].astype(F32)

        other = rows_of(sid(xo, y))
        p[k][other, :] = summed(xo).astype(BF16)
        send(p[k].at[other], rx[k], x_s.at[k], x_r.at[k], xl_dev)
        qs[k][...] = summed(xl)

    def grad_block(k, x_, y_):
        return dg[k].at[rows_of(sid(x_, y_))]

    def stage_e(k):
        wait(rx[k], x_r.at[k])
        val = (qs[k][...] + rx[k][...].astype(F32)).T
        pieces = []
        for t in range(TILES[k]):
            units = slice((FIRST[k] + t) * UNITS, (FIRST[k] + t + 1) * UNITS)
            gate, upval = val[t * 128:t * 128 + UNITS], val[t * 128 + UNITS:(t + 1) * 128]
            sigma = 1.0 / (1.0 + jnp.exp(-gate))
            active = gate * sigma
            hidden_ref[units] = (active * upval).astype(BF16)
            dh = jnp.where(live, upstream_ref[units].astype(F32), 0.0)
            pieces += [dh * upval * sigma * (1.0 + gate * (1.0 - sigma)), dh * active]
        dg[k][rows_of(sec), :] = jnp.concatenate(pieces, 0).T.astype(BF16)
        ref = grad_block(k, xl, y)
        for slot, dev in ((0, xl_dev), (1, up_dev), (2, down_dev)):
            send(ref, ref, g_s.at[k, slot], g_r.at[k, slot], dev)

    def stage_g(k):
        ref = grad_block(k, xo, y)
        wait(ref, g_r.at[k, 0])
        send(ref, ref, g_s.at[k, 3], g_r.at[k, 3], up_dev)
        send(ref, ref, g_s.at[k, 4], g_r.at[k, 4], down_dev)

    def stage_k(k):
        ref = grad_block(k, xl, ym)
        wait(ref, g_r.at[k, 1])
        send(ref, ref, g_s.at[k, 5], g_r.at[k, 5], up_dev)
        ref = grad_block(k, xo, yp)
        wait(ref, g_r.at[k, 4])
        send(ref, ref, g_s.at[k, 6], g_r.at[k, 6], down_dev)

    def stage_h(k):
        wait(grad_block(k, xl, yp), g_r.at[k, 2])
        wait(grad_block(k, xo, ym), g_r.at[k, 3])
        wait(grad_block(k, xl, yo), g_r.at[k, 5])
        wait(grad_block(k, xo, yo), g_r.at[k, 6])

        acc[:, 0:128 * TILES[k]] = jnp.dot(st_buf[...], dg[k][...], preferred_element_type=F32)

        @pl.loop(0, KDIM // 256)
        def _(i):
            cols = cols_of(i)
            turned = acc[cols, 0:128 * TILES[k]].T
            for t in range(TILES[k]):
                low, high = slice(t * 128, t * 128 + UNITS), slice(t * 128 + UNITS, (t + 1) * 128)
                units = slice((FIRST[k] + t) * UNITS, (FIRST[k] + t + 1) * UNITS)
                new_gate_ref[units, cols] = (wt[k][low, cols].astype(F32) - scale * turned[low]).astype(BF16)
                new_up_ref[units, cols] = (wt[k][high, cols].astype(F32) - scale * turned[high]).astype(BF16)

    run = {"F": stage_f, "B": stage_b, "X": stage_x, "E": stage_e, "G": stage_g, "K": stage_k, "H": stage_h}
    order = sorted((LAG * k + n, -n, name, k) for k in range(NC) for n, name in enumerate(STAGES))
    for _, _, name, k in order:
        run[name](k)
        if name == "F" and k == 0:
            @pl.loop(0, NSEC)
            def _(i):
                r = cols_of(i)
                st_buf[:, r] = s_buf[r, :].T

    @pl.when(sec != 0)
    def _():
        wait(mid, mid_s.at[0])

    @pl.when(goal != sec)
    def _():
        wait(mid, mid_s.at[1])

    for k in range(NC):
        wait(ws[k].at[pl.ds(0, NSHARD - 1)], w_s.at[k])
    for src, ss in sent:
        wait(src, ss)


def shards(states, lengths, gate_weight, up_weight, upstream):
    vmem = pl.BlockSpec(memory_space=pltpu.VMEM)
    dma = pltpu.SemaphoreType.DMA
    buffers = [
        pltpu.VMEM((ROWS, 256), BF16), pltpu.VMEM((NSEC * ROWS, KDIM), BF16), pltpu.VMEM((KDIM, NSEC * ROWS), BF16),
        pltpu.VMEM((KDIM, 128 * max(TILES)), F32),
    ]
    sizes = [128 * t for t in TILES]
    for shape, kind in (
        (lambda n: (NSHARD, DEPTH, n), BF16), (lambda n: (KDIM, n), BF16), (lambda n: (n, KDIM), BF16),
        (lambda n: (NSEC * ROWS, n), BF16), (lambda n: (2, ROWS, n), BF16), (lambda n: (4, ROWS, n), BF16),
        (lambda n: (ROWS, n), F32), (lambda n: (ROWS, n), BF16), (lambda n: (NSEC * ROWS, n), BF16),
    ):
        buffers += [pltpu.VMEM(shape(n), kind) for n in sizes]
    sems = [dma((2,)), dma((2,)), dma((2, 4)), dma((2, 4)), dma((2, 2)), dma((2, 2)), dma((5,)), dma((5,)), dma((2, 8)), dma((2, 8)),
            dma((NC,)), dma((NC,)), dma((NC, 2)), dma((NC, 2)), dma((NC, 4)), dma((NC, 4)), dma((NC,)), dma((NC,)),
            dma((NC, 7)), dma((NC, 7))]
    hidden, new_gate, new_up = pl.pallas_call(
        kernel,
        out_shape=(
            jax.ShapeDtypeStruct((WIDTH, ROWS), BF16),
            jax.ShapeDtypeStruct((WIDTH, KDIM), BF16),
            jax.ShapeDtypeStruct((WIDTH, KDIM), BF16),
        ),
        in_specs=[pl.BlockSpec(memory_space=pltpu.SMEM)] + [vmem] * 4,
        out_specs=(vmem, vmem, vmem),
        scratch_shapes=buffers + sems,
        compiler_params=pltpu.CompilerParams(collective_id=0, has_side_effects=True, vmem_limit_bytes=44 << 20),
        cost_estimate=pl.CostEstimate(flops=7516192768, bytes_accessed=8 << 20, transcendentals=ROWS * WIDTH),
        name="projection_pair",
    )(lengths, states, gate_weight, up_weight, upstream.T)
    return hidden.T, new_gate.T, new_up.T


def solution(mesh):
    in_specs = (
        P("section", "shard"),
        P(),
        P(("section", "shard"), None),
        P(("section", "shard"), None),
        P("section", "shard"),
    )
    out_specs = (P("section", "shard"), P("section", "shard"), P("section", "shard"))
    return jax.shard_map(shards, mesh=mesh, in_specs=in_specs, out_specs=out_specs, check_vma=False)
```

```python
import jax
import jax.numpy as jnp
from jax import lax
from jax.experimental import pallas as pl
from jax.experimental.pallas import tpu as pltpu
from jax.sharding import PartitionSpec as P

MESH = pl.DeviceIdType.MESH
BF16 = jnp.bfloat16
F32 = jnp.float32
NY, NX, NZ = 4, 2, 8
NSEC, NSHARD = 8, 32
ROWS = 256
HALF = ROWS // 2
DEPTH = 32
WIDTH = 448
KDIM = DEPTH * NSHARD
UNITS = 64
TILES = (1, 2, 2, 2)
NC = len(TILES)
FIRST = tuple(sum(TILES[:k]) for k in range(NC))
AHEAD = 2
LAG = 1
EARLY = 4
OFFSETS = (0, -1, 1, -2, 2, -3, 3, 4)
STAGES = "FBXEGKH"


def kernel(lengths_ref, states_hbm, gate_hbm, up_hbm, upstream_hbm, hidden_ref, new_gate_ref, new_up_ref, *scratch):
    it = iter(scratch)
    states_ref, gate_ref, up_ref, upstream_ref, mid, s_buf, st_buf, acc = [next(it) for _ in range(8)]
    ws, wr, wt, p, ra, rb, qs, rx, dg = [[next(it) for _ in range(NC)] for _ in range(9)]
    (in_s, mid_s, mid_r, ring_s, ring_r, far_s, far_r, xh_s, xh_r, core_s, core_r, w_s, w_r,
     a_s, a_r, b_s, b_r, x_s, x_r, g_s, g_r) = list(it)

    sec, shard = lax.axis_index("section"), lax.axis_index("shard")
    xl, y = lax.div(sec, NY), lax.rem(sec, NY)
    z, quarter = lax.div(shard, 4), lax.rem(shard, 4)
    xh, core = lax.div(quarter, 2), lax.rem(quarter, 2)
    xo = 1 - xl
    yp, ym, yo = lax.rem(y + 1, NY), lax.rem(y + NY - 1, NY), lax.rem(y + 2, NY)
    zp, zm = lax.rem(z + 1, NZ), lax.rem(z + NZ - 1, NZ)

    def sid(x_, y_):
        return x_ * NY + y_

    def shid(z_, xh_, c_):
        return z_ * 4 + xh_ * 2 + c_

    up_dev, down_dev, xl_dev = (sid(xl, yp), shard), (sid(xl, ym), shard), (sid(xo, y), shard)
    zp_dev, zm_dev = (sec, shid(zp, xh, core)), (sec, shid(zm, xh, core))
    core_dev, xh_dev = (sec, shid(z, xh, 1 - core)), (sec, shid(z, 1 - xh, core))

    def crossed(z_):
        out = 0
        for bit in (1, 2, 4):
            one, two = lax.rem(lax.div(z_, bit), 2), lax.rem(lax.div(sec, bit), 2)
            out = out + bit * (one + two - 2 * one * two)
        return out

    goal = crossed(z)
    mid_dev = (sec, shid(goal, xh, core))

    barrier = pltpu.get_barrier_semaphore()

    @pl.loop(1, NSEC)
    def _(d):
        to = lax.rem(sec + d, NSEC)
        pl.semaphore_signal(barrier, inc=1, device_id=(to, shard), device_id_type=MESH)

    @pl.loop(1, NSHARD)
    def _(d):
        pl.semaphore_signal(barrier, inc=1, device_id=(sec, lax.rem(shard + d, NSHARD)), device_id_type=MESH)

    loads = [
        pltpu.make_async_copy(src, dst, in_s.at[i])
        for i, (src, dst) in enumerate((
            (states_hbm, states_ref), (gate_hbm, gate_ref), (up_hbm, up_ref), (upstream_hbm, upstream_ref),
        ))
    ]
    for copy in loads:
        copy.start()

    sent = []

    def send(src, dst, ss, rs, dev):
        pltpu.make_async_remote_copy(
            src_ref=src, dst_ref=dst, send_sem=ss, recv_sem=rs, device_id=dev, device_id_type=MESH
        ).start()
        sent.append((src, ss))

    def wait(ref, sem):
        pltpu.make_async_copy(ref, ref, sem).wait()

    def slot_of(section):
        return lax.rem(section, NY) * NX + lax.div(section, NY)

    def rows_of(section):
        return pl.ds(pl.multiple_of(slot_of(section) * ROWS, ROWS), ROWS)

    def pair_of(y_):
        return pl.ds(pl.multiple_of(y_ * NX * ROWS, NX * ROWS), NX * ROWS)

    def cols_of(qq):
        return pl.ds(pl.multiple_of(qq * 256, 256), 256)

    own_rows = pl.ds(pl.multiple_of(shard * DEPTH, DEPTH), DEPTH)

    def send_weights(k):
        @pl.loop(0, NSHARD - 1)
        def _(i):
            half = lax.div(i, 2) + 1
            d = jnp.where(lax.rem(i, 2) == 0, half, NSHARD - half)
            to = lax.rem(shard + d, NSHARD)
            pltpu.make_async_remote_copy(
                src_ref=ws[k].at[to], dst_ref=wr[k].at[own_rows], send_sem=w_s.at[k], recv_sem=w_r.at[k],
                device_id=(sec, to), device_id_type=MESH,
            ).start()

        pltpu.make_async_copy(ws[k].at[shard], wr[k].at[own_rows], w_r.at[k]).start()

    loads[0].wait()
    pl.semaphore_wait(barrier, NSHARD - 1 + NSEC - 1)

    for h in range(2):
        part = pl.ds(h * HALF, HALF)

        @pl.when(sec != 0)
        def _():
            pltpu.make_async_remote_copy(
                src_ref=states_ref.at[part], dst_ref=mid.at[part], send_sem=mid_s.at[0, h], recv_sem=mid_r.at[0, h],
                device_id=mid_dev, device_id_type=MESH,
            ).start()

        @pl.when(sec == 0)
        def _():
            pltpu.make_async_copy(states_ref.at[part], mid.at[part], mid_r.at[0, h]).start()

    lane = lax.broadcasted_iota(jnp.int32, (DEPTH, 128), 1)
    loads[1].wait()
    loads[2].wait()

    @pl.loop(0, NSHARD // 2)
    def _(m):
        for k in range(NC):
            for t in range(TILES[k]):
                for odd in range(2):
                    a = odd * (WIDTH // UNITS) + FIRST[k] + t
                    cols = pl.ds(pl.multiple_of(m * 2 * WIDTH + (a // 2) * 128, 128), 128)
                    g, u = gate_ref[:, cols].astype(F32), up_ref[:, cols].astype(F32)
                    if a % 2:
                        val = jnp.where(lane < UNITS, pltpu.roll(g, UNITS, 1), u)
                    else:
                        val = jnp.where(lane < UNITS, g, pltpu.roll(u, UNITS, 1))
                    ws[k][2 * m + odd, :, t * 128:(t + 1) * 128] = val.astype(BF16)

    def half_of(section, h, qq):
        start = slot_of(section) * ROWS + h * HALF
        return s_buf.at[pl.ds(pl.multiple_of(start, HALF), HALF), cols_of(qq)]

    def piece(i, h, qq):
        return half_of(crossed(lax.rem(z + OFFSETS[i] + NZ, NZ)), h, qq)

    partner = (1 - xh) * 2 + core
    z_devs = (zp_dev, zm_dev)

    def share(i, h, part):
        ref = piece(i, h, (quarter, partner)[part])
        if part == 0 and i < 5:
            send(ref, ref, xh_s.at[i, h], xh_r.at[i, h], xh_dev)
        send(ref, ref, core_s.at[part, i, h], core_r.at[part, i, h], core_dev)

    def onward(i, h, way, qq, ss, rs):
        ref = piece(i, h, qq)
        send(ref, ref, ss, rs, z_devs[way])

    def near(i):
        for h in range(2):
            wait(piece(i, h, partner), xh_r.at[i, h])
            if i > 2:
                onward(i, h, i - 3, partner, far_s.at[i - 3, 0, h], far_r.at[i - 3, 0, h])
            share(i, h, 1)

    send_weights(0)
    for h in range(2):
        part = pl.ds(h * HALF, HALF)
        wait(mid.at[part], mid_r.at[0, h])
        to_rows = half_of(sec, h, quarter)

        @pl.when(goal != sec)
        def _():
            pltpu.make_async_remote_copy(
                src_ref=mid.at[part], dst_ref=to_rows, send_sem=mid_s.at[1, h], recv_sem=mid_r.at[1, h],
                device_id=(goal, shard), device_id_type=MESH,
            ).start()

        @pl.when(goal == sec)
        def _():
            pltpu.make_async_copy(mid.at[part], to_rows, mid_r.at[1, h]).start()

    for h in range(2):
        wait(piece(0, h, quarter), mid_r.at[1, h])
        for way in range(2):
            onward(0, h, way, quarter, ring_s.at[way, 0, h], ring_r.at[way, 0, h])
        share(0, h, 0)
    for t in range(1, 4):
        for h in range(2):
            for way in range(2):
                i = 2 * t - 1 + way
                wait(piece(i, h, quarter), ring_r.at[way, t - 1, h])
                if t < 3 or h == way:
                    onward(i, h, way, quarter, ring_s.at[way, t, h], ring_r.at[way, t, h])
                share(i, h, 0)
        if t == EARLY:
            for k in range(1, AHEAD):
                send_weights(k)
        for i in ((0,), (1, 2), (3, 4))[t - 1]:
            near(i)
    for way in range(2):
        wait(piece(7, way, quarter), ring_r.at[way, 3, way])
        share(7, way, 0)
    for h in range(2):
        for way in range(2):
            wait(piece(5 + way, h, partner), far_r.at[way, 0, h])
            if h == way:
                onward(5 + way, h, way, partner, far_s.at[way, 1, h], far_r.at[way, 1, h])
            share(5 + way, h, 1)
    if EARLY == 4:
        for k in range(1, AHEAD):
            send_weights(k)
    for way in range(2):
        wait(piece(7, way, partner), far_r.at[way, 1, way])
        share(7, way, 1)
    for part in range(2):
        for i in range(8):
            for h in range(2):
                wait(piece(i, h, (quarter, partner)[part] + 1 - 2 * core), core_r.at[part, i, h])

    loads[3].wait()
    total = lengths_ref[0]
    for i in range(1, NSEC):
        total = total + lengths_ref[i]
    live = lax.broadcasted_iota(jnp.int32, (UNITS, ROWS), 1) < lengths_ref[sec]
    scale = 0.5 / jnp.full((UNITS, 256), total.astype(F32), F32)

    def forward(k, y_):
        p[k][pair_of(y_), :] = jnp.dot(s_buf[pair_of(y_), :], wr[k][...], preferred_element_type=F32).astype(BF16)

    def part(k, x_, y_):
        return p[k].at[rows_of(sid(x_, y_))]

    def stage_f(k):
        wait(wr[k], w_r.at[k])
        if k + AHEAD < NC:
            send_weights(k + AHEAD)

        forward(k, yo)
        send(part(k, 0, yo), ra[k].at[0], a_s.at[k, 0], a_r.at[k, 0], up_dev)
        send(part(k, 1, yo), ra[k].at[1], a_s.at[k, 1], a_r.at[k, 1], down_dev)
        forward(k, yp)
        send(part(k, 1, yp), rb[k].at[1], b_s.at[k, 1], b_r.at[k, 1], up_dev)
        forward(k, ym)
        send(part(k, 0, ym), rb[k].at[2], b_s.at[k, 2], b_r.at[k, 2], down_dev)
        forward(k, y)

        @pl.loop(0, KDIM // 256)
        def _(i):
            wt[k][:, cols_of(i)] = wr[k][cols_of(i), :].T

    def stage_b(k):
        for way in range(2):
            wait(ra[k].at[way], a_r.at[k, way])
            r = rows_of(sid(way, (yp, ym)[way]))
            p[k][r, :] = (p[k][r, :].astype(F32) + ra[k][way].astype(F32)).astype(BF16)
            slot = (0, 3)[way]
            send(p[k].at[r], rb[k].at[slot], b_s.at[k, slot], b_r.at[k, slot], (up_dev, down_dev)[way])

    def stage_x(k):
        for slot in range(4):
            wait(rb[k].at[slot], b_r.at[k, slot])

        def summed(x_):
            r = rows_of(sid(x_, y))
            return p[k][r, :].astype(F32) + rb[k][x_].astype(F32) + rb[k][2 + x_].astype(F32)

        other = rows_of(sid(xo, y))
        p[k][other, :] = summed(xo).astype(BF16)
        send(p[k].at[other], rx[k], x_s.at[k], x_r.at[k], xl_dev)
        qs[k][...] = summed(xl)

    def grad_block(k, x_, y_):
        return dg[k].at[rows_of(sid(x_, y_))]

    def stage_e(k):
        wait(rx[k], x_r.at[k])
        val = (qs[k][...] + rx[k][...].astype(F32)).T
        pieces = []
        for t in range(TILES[k]):
            units = slice((FIRST[k] + t) * UNITS, (FIRST[k] + t + 1) * UNITS)
            gate, upval = val[t * 128:t * 128 + UNITS], val[t * 128 + UNITS:(t + 1) * 128]
            sigma = 1.0 / (1.0 + jnp.exp(-gate))
            active = gate * sigma
            hidden_ref[units] = (active * upval).astype(BF16)
            dh = jnp.where(live, upstream_ref[units].astype(F32), 0.0)
            pieces += [dh * upval * sigma * (1.0 + gate * (1.0 - sigma)), dh * active]
        dg[k][rows_of(sec), :] = jnp.concatenate(pieces, 0).T.astype(BF16)
        ref = grad_block(k, xl, y)
        for slot, dev in ((0, xl_dev), (1, up_dev), (2, down_dev)):
            send(ref, ref, g_s.at[k, slot], g_r.at[k, slot], dev)

    def stage_g(k):
        ref = grad_block(k, xo, y)
        wait(ref, g_r.at[k, 0])
        send(ref, ref, g_s.at[k, 3], g_r.at[k, 3], up_dev)
        send(ref, ref, g_s.at[k, 4], g_r.at[k, 4], down_dev)

    def stage_k(k):
        ref = grad_block(k, xl, ym)
        wait(ref, g_r.at[k, 1])
        send(ref, ref, g_s.at[k, 5], g_r.at[k, 5], up_dev)
        ref = grad_block(k, xo, yp)
        wait(ref, g_r.at[k, 4])
        send(ref, ref, g_s.at[k, 6], g_r.at[k, 6], down_dev)

    def stage_h(k):
        wait(grad_block(k, xl, yp), g_r.at[k, 2])
        wait(grad_block(k, xo, ym), g_r.at[k, 3])
        wait(grad_block(k, xl, yo), g_r.at[k, 5])
        wait(grad_block(k, xo, yo), g_r.at[k, 6])

        acc[:, 0:128 * TILES[k]] = jnp.dot(st_buf[...], dg[k][...], preferred_element_type=F32)

        @pl.loop(0, KDIM // 256)
        def _(i):
            cols = cols_of(i)
            turned = acc[cols, 0:128 * TILES[k]].T
            for t in range(TILES[k]):
                low, high = slice(t * 128, t * 128 + UNITS), slice(t * 128 + UNITS, (t + 1) * 128)
                units = slice((FIRST[k] + t) * UNITS, (FIRST[k] + t + 1) * UNITS)
                new_gate_ref[units, cols] = (wt[k][low, cols].astype(F32) - scale * turned[low]).astype(BF16)
                new_up_ref[units, cols] = (wt[k][high, cols].astype(F32) - scale * turned[high]).astype(BF16)

    run = {"F": stage_f, "B": stage_b, "X": stage_x, "E": stage_e, "G": stage_g, "K": stage_k, "H": stage_h}
    order = sorted((LAG * k + n, -n, name, k) for k in range(NC) for n, name in enumerate(STAGES))
    for _, _, name, k in order:
        run[name](k)
        if name == "F" and k == 0:
            @pl.loop(0, NSEC)
            def _(i):
                r = cols_of(i)
                st_buf[:, r] = s_buf[r, :].T

    @pl.when(sec != 0)
    def _():
        for h in range(2):
            wait(mid.at[pl.ds(h * HALF, HALF)], mid_s.at[0, h])

    @pl.when(goal != sec)
    def _():
        for h in range(2):
            wait(mid.at[pl.ds(h * HALF, HALF)], mid_s.at[1, h])

    for k in range(NC):
        wait(ws[k].at[pl.ds(0, NSHARD - 1)], w_s.at[k])
    for src, ss in sent:
        wait(src, ss)


def shards(states, lengths, gate_weight, up_weight, upstream):
    vmem = pl.BlockSpec(memory_space=pltpu.VMEM)
    dma = pltpu.SemaphoreType.DMA
    buffers = [
        pltpu.VMEM((ROWS, 256), BF16), pltpu.VMEM((DEPTH, WIDTH * NSHARD), BF16), pltpu.VMEM((DEPTH, WIDTH * NSHARD), BF16),
        pltpu.VMEM((WIDTH, ROWS), BF16), pltpu.VMEM((ROWS, 256), BF16), pltpu.VMEM((NSEC * ROWS, KDIM), BF16), pltpu.VMEM((KDIM, NSEC * ROWS), BF16),
        pltpu.VMEM((KDIM, 128 * max(TILES)), F32),
    ]
    sizes = [128 * t for t in TILES]
    for shape, kind in (
        (lambda n: (NSHARD, DEPTH, n), BF16), (lambda n: (KDIM, n), BF16), (lambda n: (n, KDIM), BF16),
        (lambda n: (NSEC * ROWS, n), BF16), (lambda n: (2, ROWS, n), BF16), (lambda n: (4, ROWS, n), BF16),
        (lambda n: (ROWS, n), F32), (lambda n: (ROWS, n), BF16), (lambda n: (NSEC * ROWS, n), BF16),
    ):
        buffers += [pltpu.VMEM(shape(n), kind) for n in sizes]
    sems = [dma((4,)), dma((2, 2)), dma((2, 2)), dma((2, 4, 2)), dma((2, 4, 2)), dma((2, 2, 2)), dma((2, 2, 2)), dma((5, 2)), dma((5, 2)),
            dma((2, 8, 2)), dma((2, 8, 2)),
            dma((NC,)), dma((NC,)), dma((NC, 2)), dma((NC, 2)), dma((NC, 4)), dma((NC, 4)), dma((NC,)), dma((NC,)),
            dma((NC, 7)), dma((NC, 7))]
    hidden, new_gate, new_up = pl.pallas_call(
        kernel,
        out_shape=(
            jax.ShapeDtypeStruct((WIDTH, ROWS), BF16),
            jax.ShapeDtypeStruct((WIDTH, KDIM), BF16),
            jax.ShapeDtypeStruct((WIDTH, KDIM), BF16),
        ),
        in_specs=[pl.BlockSpec(memory_space=pltpu.SMEM)] + [pl.BlockSpec(memory_space=pl.ANY)] * 4,
        out_specs=(vmem, vmem, vmem),
        scratch_shapes=buffers + sems,
        compiler_params=pltpu.CompilerParams(collective_id=0, has_side_effects=True, vmem_limit_bytes=56 << 20),
        cost_estimate=pl.CostEstimate(flops=7516192768, bytes_accessed=8 << 20, transcendentals=ROWS * WIDTH),
        name="projection_pair",
    )(lengths, states, gate_weight, up_weight, upstream.T)
    return hidden.T, new_gate.T, new_up.T


def solution(mesh):
    in_specs = (
        P("section", "shard"),
        P(),
        P(("section", "shard"), None),
        P(("section", "shard"), None),
        P("section", "shard"),
    )
    out_specs = (P("section", "shard"), P("section", "shard"), P("section", "shard"))
    return jax.shard_map(shards, mesh=mesh, in_specs=in_specs, out_specs=out_specs, check_vma=False)
```

```python
import jax
import jax.numpy as jnp
from jax import lax
from jax.experimental import pallas as pl
from jax.experimental.pallas import tpu as pltpu
from jax.sharding import PartitionSpec as P

MESH = pl.DeviceIdType.MESH
BF16 = jnp.bfloat16
F32 = jnp.float32
NY, NX, NZ = 4, 2, 8
NSEC, NSHARD = 8, 32
ROWS = 256
HALF = ROWS // 2
DEPTH = 32
WIDTH = 448
KDIM = DEPTH * NSHARD
UNITS = 64
TILES = (1, 2, 2, 2)
NC = len(TILES)
FIRST = tuple(sum(TILES[:k]) for k in range(NC))
AHEAD = 2
LAG = 1
EARLY = 4
OFFSETS = (0, -1, 1, -2, 2, -3, 3, 4)
STAGES = "FBXEGKH"


def kernel(lengths_ref, states_hbm, gate_hbm, up_hbm, upstream_hbm, hidden_ref, new_gate_ref, new_up_ref, *scratch):
    it = iter(scratch)
    states_ref, gate_ref, up_ref, upstream_ref, mid, s_buf, st_buf, acc = [next(it) for _ in range(8)]
    ws, wr, wt, p, ra, rb, qs, rx, dg = [[next(it) for _ in range(NC)] for _ in range(9)]
    (in_s, mid_s, mid_r, ring_s, ring_r, far_s, far_r, xh_s, xh_r, core_s, core_r, w_s, w_r,
     a_s, a_r, b_s, b_r, x_s, x_r, g_s, g_r) = list(it)

    sec, shard = lax.axis_index("section"), lax.axis_index("shard")
    xl, y = lax.div(sec, NY), lax.rem(sec, NY)
    z, quarter = lax.div(shard, 4), lax.rem(shard, 4)
    xh, core = lax.div(quarter, 2), lax.rem(quarter, 2)
    xo = 1 - xl
    yp, ym, yo = lax.rem(y + 1, NY), lax.rem(y + NY - 1, NY), lax.rem(y + 2, NY)
    zp, zm = lax.rem(z + 1, NZ), lax.rem(z + NZ - 1, NZ)

    def sid(x_, y_):
        return x_ * NY + y_

    def shid(z_, xh_, c_):
        return z_ * 4 + xh_ * 2 + c_

    up_dev, down_dev, xl_dev = (sid(xl, yp), shard), (sid(xl, ym), shard), (sid(xo, y), shard)
    zp_dev, zm_dev = (sec, shid(zp, xh, core)), (sec, shid(zm, xh, core))
    core_dev, xh_dev = (sec, shid(z, xh, 1 - core)), (sec, shid(z, 1 - xh, core))
    mid_dev, goal = (sec, shid(lax.rem(z + sec, NZ), xh, core)), lax.rem(z - sec + NZ, NZ)

    barrier = pltpu.get_barrier_semaphore()

    @pl.loop(1, NSEC)
    def _(d):
        to = lax.rem(sec + d, NSEC)
        pl.semaphore_signal(barrier, inc=1, device_id=(to, shard), device_id_type=MESH)

    @pl.loop(1, NSHARD)
    def _(d):
        pl.semaphore_signal(barrier, inc=1, device_id=(sec, lax.rem(shard + d, NSHARD)), device_id_type=MESH)

    loads = [
        pltpu.make_async_copy(src, dst, in_s.at[i])
        for i, (src, dst) in enumerate((
            (states_hbm, states_ref), (gate_hbm, gate_ref), (up_hbm, up_ref), (upstream_hbm, upstream_ref),
        ))
    ]
    for copy in loads:
        copy.start()

    sent = []

    def send(src, dst, ss, rs, dev):
        pltpu.make_async_remote_copy(
            src_ref=src, dst_ref=dst, send_sem=ss, recv_sem=rs, device_id=dev, device_id_type=MESH
        ).start()
        sent.append((src, ss))

    def wait(ref, sem):
        pltpu.make_async_copy(ref, ref, sem).wait()

    def slot_of(section):
        return lax.rem(section, NY) * NX + lax.div(section, NY)

    def rows_of(section):
        return pl.ds(pl.multiple_of(slot_of(section) * ROWS, ROWS), ROWS)

    def pair_of(y_):
        return pl.ds(pl.multiple_of(y_ * NX * ROWS, NX * ROWS), NX * ROWS)

    def cols_of(qq):
        return pl.ds(pl.multiple_of(qq * 256, 256), 256)

    own_rows = pl.ds(pl.multiple_of(shard * DEPTH, DEPTH), DEPTH)

    def send_weights(k):
        @pl.loop(0, NSHARD - 1)
        def _(i):
            half = lax.div(i, 2) + 1
            d = jnp.where(lax.rem(i, 2) == 0, half, NSHARD - half)
            to = lax.rem(shard + d, NSHARD)
            pltpu.make_async_remote_copy(
                src_ref=ws[k].at[to], dst_ref=wr[k].at[own_rows], send_sem=w_s.at[k], recv_sem=w_r.at[k],
                device_id=(sec, to), device_id_type=MESH,
            ).start()

        pltpu.make_async_copy(ws[k].at[shard], wr[k].at[own_rows], w_r.at[k]).start()

    loads[0].wait()
    pl.semaphore_wait(barrier, NSHARD - 1 + NSEC - 1)

    for h in range(2):
        part = pl.ds(h * HALF, HALF)

        @pl.when(sec != 0)
        def _():
            pltpu.make_async_remote_copy(
                src_ref=states_ref.at[part], dst_ref=mid.at[part], send_sem=mid_s.at[0, h], recv_sem=mid_r.at[0, h],
                device_id=mid_dev, device_id_type=MESH,
            ).start()

        @pl.when(sec == 0)
        def _():
            pltpu.make_async_copy(states_ref.at[part], mid.at[part], mid_r.at[0, h]).start()

    lane = lax.broadcasted_iota(jnp.int32, (DEPTH, 128), 1)
    loads[1].wait()
    loads[2].wait()

    @pl.loop(0, NSHARD // 2)
    def _(m):
        for k in range(NC):
            for t in range(TILES[k]):
                for odd in range(2):
                    a = odd * (WIDTH // UNITS) + FIRST[k] + t
                    cols = pl.ds(pl.multiple_of(m * 2 * WIDTH + (a // 2) * 128, 128), 128)
                    g, u = gate_ref[:, cols].astype(F32), up_ref[:, cols].astype(F32)
                    if a % 2:
                        val = jnp.where(lane < UNITS, pltpu.roll(g, UNITS, 1), u)
                    else:
                        val = jnp.where(lane < UNITS, g, pltpu.roll(u, UNITS, 1))
                    ws[k][2 * m + odd, :, t * 128:(t + 1) * 128] = val.astype(BF16)

    def half_of(section, h, qq):
        start = slot_of(section) * ROWS + h * HALF
        return s_buf.at[pl.ds(pl.multiple_of(start, HALF), HALF), cols_of(qq)]

    def piece(i, h, qq):
        return half_of(lax.rem(goal + OFFSETS[i] + NZ, NZ), h, qq)

    partner = (1 - xh) * 2 + core
    z_devs = (zp_dev, zm_dev)

    def share(i, h, part):
        ref = piece(i, h, (quarter, partner)[part])
        if part == 0 and i < 5:
            send(ref, ref, xh_s.at[i, h], xh_r.at[i, h], xh_dev)
        send(ref, ref, core_s.at[part, i, h], core_r.at[part, i, h], core_dev)

    def onward(i, h, way, qq, ss, rs):
        ref = piece(i, h, qq)
        send(ref, ref, ss, rs, z_devs[way])

    def near(i):
        for h in range(2):
            wait(piece(i, h, partner), xh_r.at[i, h])
            if i > 2:
                onward(i, h, i - 3, partner, far_s.at[i - 3, 0, h], far_r.at[i - 3, 0, h])
            share(i, h, 1)

    send_weights(0)
    for h in range(2):
        part = pl.ds(h * HALF, HALF)
        wait(mid.at[part], mid_r.at[0, h])
        to_rows = half_of(sec, h, quarter)

        @pl.when(goal != sec)
        def _():
            pltpu.make_async_remote_copy(
                src_ref=mid.at[part], dst_ref=to_rows, send_sem=mid_s.at[1, h], recv_sem=mid_r.at[1, h],
                device_id=(goal, shard), device_id_type=MESH,
            ).start()

        @pl.when(goal == sec)
        def _():
            pltpu.make_async_copy(mid.at[part], to_rows, mid_r.at[1, h]).start()

    for h in range(2):
        wait(piece(0, h, quarter), mid_r.at[1, h])
        for way in range(2):
            onward(0, h, way, quarter, ring_s.at[way, 0, h], ring_r.at[way, 0, h])
        share(0, h, 0)
    for t in range(1, 4):
        for h in range(2):
            for way in range(2):
                i = 2 * t - 1 + way
                wait(piece(i, h, quarter), ring_r.at[way, t - 1, h])
                if t < 3 or h == way:
                    onward(i, h, way, quarter, ring_s.at[way, t, h], ring_r.at[way, t, h])
                share(i, h, 0)
        if t == EARLY:
            for k in range(1, AHEAD):
                send_weights(k)
        for i in ((0,), (1, 2), (3, 4))[t - 1]:
            near(i)
    for way in range(2):
        wait(piece(7, way, quarter), ring_r.at[way, 3, way])
        share(7, way, 0)
    for h in range(2):
        for way in range(2):
            wait(piece(5 + way, h, partner), far_r.at[way, 0, h])
            if h == way:
                onward(5 + way, h, way, partner, far_s.at[way, 1, h], far_r.at[way, 1, h])
            share(5 + way, h, 1)
    if EARLY == 4:
        for k in range(1, AHEAD):
            send_weights(k)
    for way in range(2):
        wait(piece(7, way, partner), far_r.at[way, 1, way])
        share(7, way, 1)
    for part in range(2):
        for i in range(8):
            for h in range(2):
                wait(piece(i, h, (quarter, partner)[part] + 1 - 2 * core), core_r.at[part, i, h])

    loads[3].wait()
    total = lengths_ref[0]
    for i in range(1, NSEC):
        total = total + lengths_ref[i]
    live = lax.broadcasted_iota(jnp.int32, (UNITS, ROWS), 1) < lengths_ref[sec]
    scale = 0.5 / jnp.full((UNITS, 256), total.astype(F32), F32)

    def forward(k, y_):
        p[k][pair_of(y_), :] = jnp.dot(s_buf[pair_of(y_), :], wr[k][...], preferred_element_type=F32).astype(BF16)

    def part(k, x_, y_):
        return p[k].at[rows_of(sid(x_, y_))]

    def stage_f(k):
        wait(wr[k], w_r.at[k])
        if k + AHEAD < NC:
            send_weights(k + AHEAD)

        forward(k, yo)
        send(part(k, 0, yo), ra[k].at[0], a_s.at[k, 0], a_r.at[k, 0], up_dev)
        send(part(k, 1, yo), ra[k].at[1], a_s.at[k, 1], a_r.at[k, 1], down_dev)
        forward(k, yp)
        send(part(k, 1, yp), rb[k].at[1], b_s.at[k, 1], b_r.at[k, 1], up_dev)
        forward(k, ym)
        send(part(k, 0, ym), rb[k].at[2], b_s.at[k, 2], b_r.at[k, 2], down_dev)
        forward(k, y)

        @pl.loop(0, KDIM // 256)
        def _(i):
            wt[k][:, cols_of(i)] = wr[k][cols_of(i), :].T

    def stage_b(k):
        for way in range(2):
            wait(ra[k].at[way], a_r.at[k, way])
            r = rows_of(sid(way, (yp, ym)[way]))
            p[k][r, :] = (p[k][r, :].astype(F32) + ra[k][way].astype(F32)).astype(BF16)
            slot = (0, 3)[way]
            send(p[k].at[r], rb[k].at[slot], b_s.at[k, slot], b_r.at[k, slot], (up_dev, down_dev)[way])

    def stage_x(k):
        for slot in range(4):
            wait(rb[k].at[slot], b_r.at[k, slot])

        def summed(x_):
            r = rows_of(sid(x_, y))
            return p[k][r, :].astype(F32) + rb[k][x_].astype(F32) + rb[k][2 + x_].astype(F32)

        other = rows_of(sid(xo, y))
        p[k][other, :] = summed(xo).astype(BF16)
        send(p[k].at[other], rx[k], x_s.at[k], x_r.at[k], xl_dev)
        qs[k][...] = summed(xl)

    def grad_block(k, x_, y_):
        return dg[k].at[rows_of(sid(x_, y_))]

    def stage_e(k):
        wait(rx[k], x_r.at[k])
        val = (qs[k][...] + rx[k][...].astype(F32)).T
        pieces = []
        for t in range(TILES[k]):
            units = slice((FIRST[k] + t) * UNITS, (FIRST[k] + t + 1) * UNITS)
            gate, upval = val[t * 128:t * 128 + UNITS], val[t * 128 + UNITS:(t + 1) * 128]
            sigma = 1.0 / (1.0 + jnp.exp(-gate))
            active = gate * sigma
            hidden_ref[units] = (active * upval).astype(BF16)
            dh = jnp.where(live, upstream_ref[units].astype(F32), 0.0)
            pieces += [dh * upval * sigma * (1.0 + gate * (1.0 - sigma)), dh * active]
        dg[k][rows_of(sec), :] = jnp.concatenate(pieces, 0).T.astype(BF16)
        ref = grad_block(k, xl, y)
        for slot, dev in ((0, xl_dev), (1, up_dev), (2, down_dev)):
            send(ref, ref, g_s.at[k, slot], g_r.at[k, slot], dev)

    def stage_g(k):
        ref = grad_block(k, xo, y)
        wait(ref, g_r.at[k, 0])
        send(ref, ref, g_s.at[k, 3], g_r.at[k, 3], up_dev)
        send(ref, ref, g_s.at[k, 4], g_r.at[k, 4], down_dev)

    def stage_k(k):
        ref = grad_block(k, xl, ym)
        wait(ref, g_r.at[k, 1])
        send(ref, ref, g_s.at[k, 5], g_r.at[k, 5], up_dev)
        ref = grad_block(k, xo, yp)
        wait(ref, g_r.at[k, 4])
        send(ref, ref, g_s.at[k, 6], g_r.at[k, 6], down_dev)

    def stage_h(k):
        wait(grad_block(k, xl, yp), g_r.at[k, 2])
        wait(grad_block(k, xo, ym), g_r.at[k, 3])
        wait(grad_block(k, xl, yo), g_r.at[k, 5])
        wait(grad_block(k, xo, yo), g_r.at[k, 6])

        acc[:, 0:128 * TILES[k]] = jnp.dot(st_buf[...], dg[k][...], preferred_element_type=F32)

        @pl.loop(0, KDIM // 256)
        def _(i):
            cols = cols_of(i)
            turned = acc[cols, 0:128 * TILES[k]].T
            for t in range(TILES[k]):
                low, high = slice(t * 128, t * 128 + UNITS), slice(t * 128 + UNITS, (t + 1) * 128)
                units = slice((FIRST[k] + t) * UNITS, (FIRST[k] + t + 1) * UNITS)
                new_gate_ref[units, cols] = (wt[k][low, cols].astype(F32) - scale * turned[low]).astype(BF16)
                new_up_ref[units, cols] = (wt[k][high, cols].astype(F32) - scale * turned[high]).astype(BF16)

    run = {"F": stage_f, "B": stage_b, "X": stage_x, "E": stage_e, "G": stage_g, "K": stage_k, "H": stage_h}
    order = sorted((LAG * k + n, -n, name, k) for k in range(NC) for n, name in enumerate(STAGES))
    for _, _, name, k in order:
        run[name](k)
        if name == "F" and k == 0:
            @pl.loop(0, NSEC)
            def _(i):
                r = cols_of(i)
                st_buf[:, r] = s_buf[r, :].T

    @pl.when(sec != 0)
    def _():
        for h in range(2):
            wait(mid.at[pl.ds(h * HALF, HALF)], mid_s.at[0, h])

    @pl.when(goal != sec)
    def _():
        for h in range(2):
            wait(mid.at[pl.ds(h * HALF, HALF)], mid_s.at[1, h])

    for k in range(NC):
        wait(ws[k].at[pl.ds(0, NSHARD - 1)], w_s.at[k])
    for src, ss in sent:
        wait(src, ss)


def shards(states, lengths, gate_weight, up_weight, upstream):
    vmem = pl.BlockSpec(memory_space=pltpu.VMEM)
    dma = pltpu.SemaphoreType.DMA
    buffers = [
        pltpu.VMEM((ROWS, 256), BF16), pltpu.VMEM((DEPTH, WIDTH * NSHARD), BF16), pltpu.VMEM((DEPTH, WIDTH * NSHARD), BF16),
        pltpu.VMEM((WIDTH, ROWS), BF16), pltpu.VMEM((ROWS, 256), BF16), pltpu.VMEM((NSEC * ROWS, KDIM), BF16), pltpu.VMEM((KDIM, NSEC * ROWS), BF16),
        pltpu.VMEM((KDIM, 128 * max(TILES)), F32),
    ]
    sizes = [128 * t for t in TILES]
    for shape, kind in (
        (lambda n: (NSHARD, DEPTH, n), BF16), (lambda n: (KDIM, n), BF16), (lambda n: (n, KDIM), BF16),
        (lambda n: (NSEC * ROWS, n), BF16), (lambda n: (2, ROWS, n), BF16), (lambda n: (4, ROWS, n), BF16),
        (lambda n: (ROWS, n), F32), (lambda n: (ROWS, n), BF16), (lambda n: (NSEC * ROWS, n), BF16),
    ):
        buffers += [pltpu.VMEM(shape(n), kind) for n in sizes]
    sems = [dma((4,)), dma((2, 2)), dma((2, 2)), dma((2, 4, 2)), dma((2, 4, 2)), dma((2, 2, 2)), dma((2, 2, 2)), dma((5, 2)), dma((5, 2)),
            dma((2, 8, 2)), dma((2, 8, 2)),
            dma((NC,)), dma((NC,)), dma((NC, 2)), dma((NC, 2)), dma((NC, 4)), dma((NC, 4)), dma((NC,)), dma((NC,)),
            dma((NC, 7)), dma((NC, 7))]
    hidden, new_gate, new_up = pl.pallas_call(
        kernel,
        out_shape=(
            jax.ShapeDtypeStruct((WIDTH, ROWS), BF16),
            jax.ShapeDtypeStruct((WIDTH, KDIM), BF16),
            jax.ShapeDtypeStruct((WIDTH, KDIM), BF16),
        ),
        in_specs=[pl.BlockSpec(memory_space=pltpu.SMEM)] + [pl.BlockSpec(memory_space=pl.ANY)] * 4,
        out_specs=(vmem, vmem, vmem),
        scratch_shapes=buffers + sems,
        compiler_params=pltpu.CompilerParams(collective_id=0, has_side_effects=True, vmem_limit_bytes=56 << 20),
        cost_estimate=pl.CostEstimate(flops=7516192768, bytes_accessed=8 << 20, transcendentals=ROWS * WIDTH),
        name="projection_pair",
    )(lengths, states, gate_weight, up_weight, upstream.T)
    return hidden.T, new_gate.T, new_up.T


def solution(mesh):
    in_specs = (
        P("section", "shard"),
        P(),
        P(("section", "shard"), None),
        P(("section", "shard"), None),
        P("section", "shard"),
    )
    out_specs = (P("section", "shard"), P("section", "shard"), P("section", "shard"))
    return jax.shard_map(shards, mesh=mesh, in_specs=in_specs, out_specs=out_specs, check_vma=False)
```
